32 devices in a mesh: chan: 8 (over z, y), inp: 4 (over x, core).
Axes of the slice: x: 2, y: 2, z: 4, core: 2. Of those that a mesh axis runs over, the one named last changes fastest.
Arguments:
- voltages: int32 [512, 131072], P('inp', 'chan'), may hold values from -128 to 127
- scales: int32 [512], P('inp'), may hold values from 1 to 5
Outputs:
- visibilities: bfloat16 [2, 1024, 512, 512], P(None, 'chan', 'inp')
The draws below stay inside these ranges and needn't reach their ends.
All inputs are finite; a program needn't handle non-finite values.
Results may differ from the reference program's by a relative error of at most 0.0069.
Values may be sent and summed in bfloat16 or wider, within the bound.
A program may use at most 192 MiB of HBM per device.

```python
import math
import jax
import jax.numpy as jnp
from jax import lax

INPUTS = 512
NFFT = 4096
CHANS = 1024
TAPS = 8
SPECTRA = 32


def touch_ends(values, stream_key, low, largest):
    shape = values.shape
    place = [jax.random.randint(jax.random.fold_in(stream_key, axis), (), 0, shape[axis]) for axis in range(len(shape))]
    values = values.at[tuple(place)].set(low)
    longest = shape.index(max(shape))
    place[longest] = (place[longest] + 1) % shape[longest]
    return values.at[tuple(place)].set(largest)


def setup_inputs(seed: int = 0) -> dict:
    key_of = jax.random.split(jax.random.key(seed), 3)
    return {
        "voltages": touch_ends(jax.random.randint(key_of[0], (INPUTS, SPECTRA * NFFT), -128, 128), jax.random.fold_in(key_of[0], 1), -128, 127).astype(jnp.int32),
        "scales": touch_ends(jax.random.randint(key_of[1], (INPUTS,), 1, 6), jax.random.fold_in(key_of[1], 1), 1, 5).astype(jnp.int32),
    }


def window_table():
    count = TAPS * NFFT
    places = jnp.arange(count).astype(jnp.float32)
    shaping = jnp.sinc((places - count / 2.0) / NFFT)
    taper = 0.5 - 0.5 * jnp.cos(2.0 * math.pi * places / count)
    return (shaping * taper).reshape(TAPS, NFFT)

def dft_table():
    columns = jnp.arange(CHANS, dtype=jnp.int32)
    norm_factor = 1.0 / math.sqrt(NFFT)

    def one_block(start):
        rows_idx = start + jnp.arange(512, dtype=jnp.int32)
        phase = rows_idx[:, None] * columns[None, :] % NFFT
        angle = phase.astype(jnp.float32) * (2.0 * math.pi / NFFT)
        return jnp.stack([jnp.cos(angle) * norm_factor, -jnp.sin(angle) * norm_factor], axis=1).astype(jnp.bfloat16)
    starts = jnp.arange(NFFT // 512, dtype=jnp.int32) * 512
    return lax.map(one_block, starts).reshape(NFFT, 2, CHANS)

def filter_taps(padded, window, spec_count):
    total = jnp.zeros((padded.shape[0], spec_count, NFFT), jnp.float32)
    for tap_index in range(TAPS):
        total = total + window[tap_index] * padded[:, tap_index:tap_index + spec_count]
    return total.astype(jnp.bfloat16)

def reference(voltages, scales):
    window = window_table()
    table = dft_table()
    group = 32
    volt_groups = voltages.reshape(INPUTS // group, group, SPECTRA, NFFT)
    scale_groups = scales.reshape(INPUTS // group, group)

    def one_group(operands):
        volt_block, scale_block = operands
        signal = volt_block.astype(jnp.float32) * scale_block.astype(jnp.float32)[:, None, None] * (1.0 / 256.0)
        padded = jnp.concatenate([jnp.zeros((group, TAPS - 1, NFFT), jnp.float32), signal], axis=1)
        filtered = filter_taps(padded, window, SPECTRA)
        return jnp.einsum('isn,nrc->cirs', filtered.astype(jnp.float32), table.astype(jnp.float32)).astype(jnp.bfloat16)
    parts = lax.map(one_group, (volt_groups, scale_groups))
    spectra = jnp.moveaxis(parts, 0, 1).reshape(CHANS, INPUTS, 2 * SPECTRA)
    blocks = spectra.reshape(CHANS // 8, 8, INPUTS, 2 * SPECTRA)

    def correlate(block):
        values = block.astype(jnp.float32)
        swapped = jnp.concatenate([values[..., SPECTRA:], -values[..., :SPECTRA]], axis=-1)
        real_part = jnp.einsum('cik,cjk->cij', values, values) * (1.0 / SPECTRA)
        imag_part = jnp.einsum('cik,cjk->cij', swapped, values) * (1.0 / SPECTRA)
        return (real_part.astype(jnp.bfloat16), imag_part.astype(jnp.bfloat16))
    real_all, imag_all = lax.map(correlate, blocks)
    return jnp.stack([real_all.reshape(CHANS, INPUTS, INPUTS), imag_all.reshape(CHANS, INPUTS, INPUTS)])
```

```python
import math

import jax
import jax.numpy as jnp
import ml_dtypes
import numpy as np
from jax import lax
from jax.experimental import pallas as pl
from jax.experimental.pallas import tpu as pltpu
from jax.sharding import PartitionSpec as P

NFFT = 4096
CHANS = 1024
TAPS = 8
MESH = pl.DeviceIdType.MESH


def shifted(block, axis, distance):
    devices = range(lax.axis_size(axis))
    route = [(i - distance, i) for i in devices if i - distance in devices]
    return lax.ppermute(block, axis, route)


def window_table():
    count = TAPS * NFFT
    places = jnp.arange(count).astype(jnp.float32)
    shaping = jnp.sinc((places - count / 2.0) / NFFT)
    taper = 0.5 - 0.5 * jnp.cos(2.0 * math.pi * places / count)
    return (shaping * taper).reshape(TAPS, NFFT)


def dft_table():
    columns = jnp.arange(CHANS, dtype=jnp.int32)
    norm_factor = 1.0 / math.sqrt(NFFT)

    def one_block(start):
        rows_idx = start + jnp.arange(512, dtype=jnp.int32)
        phase = rows_idx[:, None] * columns[None, :] % NFFT
        angle = phase.astype(jnp.float32) * (2.0 * math.pi / NFFT)
        return jnp.stack(
            [jnp.cos(angle) * norm_factor, -jnp.sin(angle) * norm_factor], axis=1
        ).astype(jnp.bfloat16)

    starts = jnp.arange(NFFT // 512, dtype=jnp.int32) * 512
    return lax.map(one_block, starts).reshape(NFFT, 2, CHANS)


def filter_taps(padded, window, spec_count):
    total = jnp.zeros((padded.shape[0], spec_count, NFFT), jnp.float32)
    for tap_index in range(TAPS):
        total = total + window[tap_index] * padded[:, tap_index : tap_index + spec_count]
    return total.astype(jnp.bfloat16)


def shards(voltages, scales):
    inp_count = voltages.shape[0]
    shard_len = voltages.shape[1]
    spec_count = shard_len // NFFT
    history_len = (TAPS - 1) * NFFT
    reach_back = -(-history_len // shard_len)
    samples = voltages.astype(jnp.bfloat16)
    earlier = []
    for distance in range(1, reach_back + 1):
        take_count = min(shard_len, history_len - (distance - 1) * shard_len)
        received = shifted(samples[:, shard_len - take_count :], "chan", distance)
        earlier = [received] + earlier
    joined = jnp.concatenate(earlier + [samples], axis=1).astype(jnp.float32)
    signal = joined * scales.astype(jnp.float32)[:, None] * (1.0 / 256.0)
    padded = signal.reshape(inp_count, TAPS - 1 + spec_count, NFFT)
    filtered = filter_taps(padded, window_table(), spec_count)
    spectra = jnp.einsum(
        "isn,nrc->cirs", filtered, dft_table(), preferred_element_type=jnp.float32
    ).astype(jnp.bfloat16)
    local_block = lax.all_to_all(spectra, "chan", split_axis=0, concat_axis=3, tiled=True)
    chan_count = local_block.shape[0]
    spec_total = local_block.shape[3]
    own_rows = local_block.reshape(chan_count, inp_count, 2 * spec_total)
    swapped = jnp.concatenate([own_rows[..., spec_total:], -own_rows[..., :spec_total]], axis=-1)
    piece = lax.all_gather(own_rows, "inp", axis=1, tiled=True)
    real_part = jnp.einsum("cik,cjk->cij", own_rows, piece, preferred_element_type=jnp.float32)
    imag_part = jnp.einsum("cik,cjk->cij", swapped, piece, preferred_element_type=jnp.float32)
    result = jnp.stack([real_part, imag_part]) * (1.0 / spec_total)
    return result.astype(jnp.bfloat16)


SUBS = 4
PART = 11


def fold_tables():
    places = np.arange(TAPS * NFFT).astype(np.float64)
    window = np.sinc((places - TAPS * NFFT / 2) / NFFT) * (0.5 - 0.5 * np.cos(2 * np.pi * places / (TAPS * NFFT)))
    window = window.reshape(TAPS, NFFT).astype(np.float32)
    edge = np.zeros((4, NFFT), np.float32)
    wide = np.concatenate([edge, window, edge], axis=0)
    m = np.arange(NFFT // 4)
    out = []
    for e in range(4):
        c = 4 * np.arange(CHANS // 4) + e
        angle = 2 * np.pi * ((m[None, :] * c[:, None]) % NFFT) / NFFT
        co, si = np.cos(angle) / 64, np.sin(angle) / 64
        if e % 2 == 0:
            re, im = co, -si
        elif e == 1:
            re, im = np.concatenate([co, -si], 1), np.concatenate([-si, -co], 1)
        else:
            re, im = np.concatenate([co, si], 1), np.concatenate([-si, co], 1)
        groups = 8
        both = np.stack([re.reshape(groups, -1, re.shape[1]), im.reshape(groups, -1, re.shape[1])], axis=1)
        out.append(both.reshape(-1, re.shape[1]).astype(ml_dtypes.bfloat16))
    return wide, np.stack([out[0], out[2]]), np.stack([out[1], out[3]])


def front_kernel(x_ref, g_ref, w_ref, even_ref, odd_ref, o_ref, y_ref):
    p = pl.program_id(0)
    rows, span, quarter = 32, 256, NFFT // 4

    for half in range(2):
        s = 2 * p + half

        @pl.loop(0, 128 // rows)
        def _(i):
            r0 = pl.multiple_of(i * rows, rows)
            gain = g_ref[pl.ds(r0, rows), :]
            for l in range(quarter // span):
                f = []
                for q in range(4):
                    acc = None
                    for b in range(4):
                        col = q * quarter + l * span
                        x = x_ref[pl.ds(r0, rows), b * NFFT + col:b * NFFT + col + span].astype(jnp.float32)
                        term = x * w_ref[b + 11 - s, :, col:col + span]
                        acc = term if acc is None else acc + term
                    f.append(acc)
                a, b2 = f[0] + f[2], f[1] + f[3]
                at = pl.ds(half * 128 + r0, rows)
                for j, v in enumerate((a + b2, a - b2, f[0] - f[2], f[1] - f[3])):
                    y_ref[at, j * quarter + l * span:j * quarter + (l + 1) * span] = (v * gain).astype(jnp.bfloat16)

    nt = (((1,), (1,)), ((), ()))
    for e in range(4):
        for part in range(2):
            sel = pl.ds(part * 256, 256)
            if e % 2 == 0:
                tab, y = even_ref[e // 2, sel, :], y_ref[:, (e // 2) * quarter:(e // 2 + 1) * quarter]
            else:
                tab, y = odd_ref[e // 2, sel, :], y_ref[:, 2 * quarter:]
            res = lax.dot_general(tab, y, nt, preferred_element_type=jnp.float32).astype(jnp.bfloat16)
            for half in range(2):
                o_ref[4 * part:4 * part + 4, e, half] = res[:, half * 128:(half + 1) * 128].reshape(4, 2, 32, 128)


def comm_kernel(p_ref, o_ref, got, own, send_sem, recv_sem, loc_sem, xsend, xrecv):
    me = lax.axis_index("chan")
    inp = lax.axis_index("inp")
    mate = inp + 1 - 2 * lax.rem(inp, 2)
    across = lax.rem(inp + 2, 4)
    barrier = pltpu.get_barrier_semaphore()
    for k in range(1, 8):
        pl.semaphore_signal(barrier, inc=1, device_id={"chan": lax.rem(me + k, 8)}, device_id_type=MESH)
    for other in (mate, across):
        pl.semaphore_signal(barrier, inc=1, device_id={"inp": other}, device_id_type=MESH)
    pl.semaphore_wait(barrier, 9)

    def turn(e, k):
        return pltpu.make_async_remote_copy(
            src_ref=p_ref.at[lax.rem(me + k, 8), e, pl.ds(0, PART)], dst_ref=got.at[me, e],
            send_sem=send_sem.at[e, k], recv_sem=recv_sem.at[e, k],
            device_id={"chan": lax.rem(me + k, 8)}, device_id_type=MESH)

    def stay(e):
        return pltpu.make_async_copy(p_ref.at[me, e, pl.ds(0, PART)], got.at[me, e], recv_sem.at[e, 0])

    def pair(e, which):
        src = own.at[e] if which < 2 else o_ref.at[across, e]
        dst = o_ref.at[inp, e] if which < 2 else o_ref.at[across, e]
        return pltpu.make_async_remote_copy(
            src_ref=src, dst_ref=dst, send_sem=xsend.at[e, which], recv_sem=xrecv.at[e, which],
            device_id={"inp": across if which == 0 else mate}, device_id_type=MESH)

    def keep(e):
        return pltpu.make_async_copy(own.at[e], o_ref.at[inp, e], loc_sem.at[e])

    for e in range(SUBS):
        for k in range(1, 8):
            turn(e, k).start()
        stay(e).start()
    for e in range(SUBS):
        stay(e).wait()
        for k in range(1, 8):
            turn(e, k).wait_recv()
        for s in range(32):
            total = None
            for src in range(max(0, s // 4 - 2), s // 4 + 1):
                if s - 4 * src < PART:
                    term = got[src, e, s - 4 * src].astype(jnp.float32)
                    total = term if total is None else total + term
            own[e, s] = total.astype(jnp.bfloat16)
        pair(e, 0).start()
        pair(e, 1).start()
        keep(e).start()
        if e:
            pair(e - 1, 0).wait_recv()
            pair(e - 1, 2).start()
    pair(SUBS - 1, 0).wait_recv()
    pair(SUBS - 1, 2).start()
    for e in range(SUBS):
        for k in range(1, 8):
            turn(e, k).wait_send()
        keep(e).wait()
        pair(e, 0).wait_send()
        pair(e, 1).wait()
        pair(e, 2).wait()


def pair_kernel(me_ref, all_ref, own_ref, o_ref):
    del me_ref
    for e in range(4):
        for d in range(2):
            own = own_ref[e, d]
            both = jnp.concatenate([jnp.concatenate([own[:32], own[32:]], axis=0),
                                    jnp.concatenate([own[32:], -own[:32]], axis=0)], axis=1)
            res = lax.dot_general(both, all_ref[e, d], (((0,), (0,)), ((), ())), preferred_element_type=jnp.float32)
            res = (res * (1.0 / 32.0)).astype(jnp.bfloat16)
            o_ref[0, 4 * d + e] = res[:128]
            o_ref[1, 4 * d + e] = res[128:]


def fast(voltages, scales):
    wide, even, odd = (jnp.asarray(t) for t in fold_tables())
    gains = (scales.astype(jnp.float32) * (1.0 / 256.0))[:, None]
    whole = lambda *shape: pl.BlockSpec(shape, lambda p: (0,) * len(shape))
    parts = pl.pallas_call(
        front_kernel, grid=(6,),
        out_shape=jax.ShapeDtypeStruct((8, 4, 12, 2, 32, 128), jnp.bfloat16),
        in_specs=[whole(128, 16384), whole(128, 1), whole(16, 1, NFFT), whole(2, 512, 1024), whole(2, 512, 2048)],
        out_specs=pl.BlockSpec((8, 4, 2, 2, 32, 128), lambda p: (0, 0, p, 0, 0, 0)),
        scratch_shapes=[pltpu.VMEM((256, NFFT), jnp.bfloat16)],
        compiler_params=pltpu.CompilerParams(vmem_limit_bytes=56 << 20),
        name="filter_transform",
    )(voltages, gains, wide[:, None], even, odd)
    gathered = pl.pallas_call(
        comm_kernel,
        out_shape=jax.ShapeDtypeStruct((4, 4, 32, 2, 32, 128), jnp.bfloat16),
        in_specs=[pl.BlockSpec(memory_space=pl.ANY)],
        out_specs=pl.BlockSpec(memory_space=pl.ANY),
        scratch_shapes=[
            pltpu.VMEM((8, SUBS, PART, 2, 32, 128), jnp.bfloat16),
            pltpu.VMEM((SUBS, 32, 2, 32, 128), jnp.bfloat16),
            pltpu.SemaphoreType.DMA((SUBS, 8)), pltpu.SemaphoreType.DMA((SUBS, 8)),
            pltpu.SemaphoreType.DMA((SUBS,)),
            pltpu.SemaphoreType.DMA((SUBS, 3)), pltpu.SemaphoreType.DMA((SUBS, 3)),
        ],
        compiler_params=pltpu.CompilerParams(
            collective_id=0, has_side_effects=True, vmem_limit_bytes=48 << 20),
        name="turn_and_share",
    )(parts)
    lined = gathered.transpose(1, 4, 3, 2, 0, 5).reshape(4, 32, 64, 512)
    me = lax.axis_index("inp").astype(jnp.int32).reshape(1)
    return pl.pallas_call(
        pair_kernel,
        out_shape=jax.ShapeDtypeStruct((2, 128, 128, 512), jnp.bfloat16),
        grid_spec=pltpu.PrefetchScalarGridSpec(
            num_scalar_prefetch=1, grid=(16,),
            in_specs=[pl.BlockSpec((4, 2, 64, 512), lambda g, m: (0, g, 0, 0)),
                      pl.BlockSpec((4, 2, 64, 128), lambda g, m: (0, g, 0, m[0]))],
            out_specs=pl.BlockSpec((2, 8, 128, 512), lambda g, m: (0, g, 0, 0))),
        compiler_params=pltpu.CompilerParams(vmem_limit_bytes=48 << 20),
        name="correlate",
    )(me, lined, lined)


def solution(mesh):
    placed = (P("inp", "chan"), P("inp"))
    sizes = (mesh.shape["chan"], mesh.shape["inp"])
    return jax.shard_map(
        fast if sizes == (8, 4) else shards,
        mesh=mesh, in_specs=placed, out_specs=P(None, "chan", "inp", None), check_vma=False
    )
```

```python
import math

import jax
import jax.numpy as jnp
import ml_dtypes
import numpy as np
from jax import lax
from jax.experimental import pallas as pl
from jax.experimental.pallas import tpu as pltpu
from jax.sharding import PartitionSpec as P

NFFT = 4096
CHANS = 1024
TAPS = 8
MESH = pl.DeviceIdType.MESH


def shifted(block, axis, distance):
    devices = range(lax.axis_size(axis))
    route = [(i - distance, i) for i in devices if i - distance in devices]
    return lax.ppermute(block, axis, route)


def window_table():
    count = TAPS * NFFT
    places = jnp.arange(count).astype(jnp.float32)
    shaping = jnp.sinc((places - count / 2.0) / NFFT)
    taper = 0.5 - 0.5 * jnp.cos(2.0 * math.pi * places / count)
    return (shaping * taper).reshape(TAPS, NFFT)


def dft_table():
    columns = jnp.arange(CHANS, dtype=jnp.int32)
    norm_factor = 1.0 / math.sqrt(NFFT)

    def one_block(start):
        rows_idx = start + jnp.arange(512, dtype=jnp.int32)
        phase = rows_idx[:, None] * columns[None, :] % NFFT
        angle = phase.astype(jnp.float32) * (2.0 * math.pi / NFFT)
        return jnp.stack(
            [jnp.cos(angle) * norm_factor, -jnp.sin(angle) * norm_factor], axis=1
        ).astype(jnp.bfloat16)

    starts = jnp.arange(NFFT // 512, dtype=jnp.int32) * 512
    return lax.map(one_block, starts).reshape(NFFT, 2, CHANS)


def filter_taps(padded, window, spec_count):
    total = jnp.zeros((padded.shape[0], spec_count, NFFT), jnp.float32)
    for tap_index in range(TAPS):
        total = total + window[tap_index] * padded[:, tap_index : tap_index + spec_count]
    return total.astype(jnp.bfloat16)


def shards(voltages, scales):
    inp_count = voltages.shape[0]
    shard_len = voltages.shape[1]
    spec_count = shard_len // NFFT
    history_len = (TAPS - 1) * NFFT
    reach_back = -(-history_len // shard_len)
    samples = voltages.astype(jnp.bfloat16)
    earlier = []
    for distance in range(1, reach_back + 1):
        take_count = min(shard_len, history_len - (distance - 1) * shard_len)
        received = shifted(samples[:, shard_len - take_count :], "chan", distance)
        earlier = [received] + earlier
    joined = jnp.concatenate(earlier + [samples], axis=1).astype(jnp.float32)
    signal = joined * scales.astype(jnp.float32)[:, None] * (1.0 / 256.0)
    padded = signal.reshape(inp_count, TAPS - 1 + spec_count, NFFT)
    filtered = filter_taps(padded, window_table(), spec_count)
    spectra = jnp.einsum(
        "isn,nrc->cirs", filtered, dft_table(), preferred_element_type=jnp.float32
    ).astype(jnp.bfloat16)
    local_block = lax.all_to_all(spectra, "chan", split_axis=0, concat_axis=3, tiled=True)
    chan_count = local_block.shape[0]
    spec_total = local_block.shape[3]
    own_rows = local_block.reshape(chan_count, inp_count, 2 * spec_total)
    swapped = jnp.concatenate([own_rows[..., spec_total:], -own_rows[..., :spec_total]], axis=-1)
    piece = lax.all_gather(own_rows, "inp", axis=1, tiled=True)
    real_part = jnp.einsum("cik,cjk->cij", own_rows, piece, preferred_element_type=jnp.float32)
    imag_part = jnp.einsum("cik,cjk->cij", swapped, piece, preferred_element_type=jnp.float32)
    result = jnp.stack([real_part, imag_part]) * (1.0 / spec_total)
    return result.astype(jnp.bfloat16)


SUBS = 4
PART = 11


def fold_tables():
    places = np.arange(TAPS * NFFT).astype(np.float64)
    window = np.sinc((places - TAPS * NFFT / 2) / NFFT) * (0.5 - 0.5 * np.cos(2 * np.pi * places / (TAPS * NFFT)))
    window = window.reshape(TAPS, NFFT).astype(np.float32)
    edge = np.zeros((4, NFFT), np.float32)
    wide = np.concatenate([edge, window, edge], axis=0)
    m = np.arange(NFFT // 4)
    out = []
    for e in range(4):
        c = 4 * np.arange(CHANS // 4) + e
        angle = 2 * np.pi * ((m[None, :] * c[:, None]) % NFFT) / NFFT
        co, si = np.cos(angle) / 64, np.sin(angle) / 64
        if e % 2 == 0:
            re, im = co, -si
        elif e == 1:
            re, im = np.concatenate([co, -si], 1), np.concatenate([-si, -co], 1)
        else:
            re, im = np.concatenate([co, si], 1), np.concatenate([-si, co], 1)
        groups = 8
        both = np.stack([re.reshape(groups, -1, re.shape[1]), im.reshape(groups, -1, re.shape[1])], axis=1)
        out.append(both.reshape(-1, re.shape[1]).astype(ml_dtypes.bfloat16))
    return wide, np.stack([out[0], out[2]]), np.stack([out[1], out[3]])


def front_kernel(x_ref, g_ref, w_ref, even_ref, odd_ref, o_ref, y_ref):
    p = pl.program_id(0)
    rows, span, quarter = 32, 256, NFFT // 4

    for half in range(2):
        s = 2 * p + half

        @pl.loop(0, 128 // rows)
        def _(i):
            r0 = pl.multiple_of(i * rows, rows)
            gain = g_ref[pl.ds(r0, rows), :]
            for l in range(quarter // span):
                f = []
                for q in range(4):
                    acc = None
                    for b in range(4):
                        col = q * quarter + l * span
                        x = x_ref[pl.ds(r0, rows), b * NFFT + col:b * NFFT + col + span].astype(jnp.float32)
                        term = x * w_ref[b + 11 - s, :, col:col + span]
                        acc = term if acc is None else acc + term
                    f.append(acc)
                a, b2 = f[0] + f[2], f[1] + f[3]
                at = pl.ds(half * 128 + r0, rows)
                for j, v in enumerate((a + b2, a - b2, f[0] - f[2], f[1] - f[3])):
                    y_ref[at, j * quarter + l * span:j * quarter + (l + 1) * span] = (v * gain).astype(jnp.bfloat16)

    nt = (((1,), (1,)), ((), ()))
    for e in range(4):
        for part in range(2):
            sel = pl.ds(part * 256, 256)
            if e % 2 == 0:
                tab, y = even_ref[e // 2, sel, :], y_ref[:, (e // 2) * quarter:(e // 2 + 1) * quarter]
            else:
                tab, y = odd_ref[e // 2, sel, :], y_ref[:, 2 * quarter:]
            res = lax.dot_general(tab, y, nt, preferred_element_type=jnp.float32).astype(jnp.bfloat16)
            for half in range(2):
                blocks = res[:, half * 128:(half + 1) * 128].reshape(2, 2, 2, 32, 128)
                for y in range(2):
                    o_ref[y, e, 2 * part:2 * part + 2, half] = blocks[:, y]


def comm_kernel(p_ref, o_ref, near, comb, got, own, ysend, yrecv, zsend, zrecv, loc_sem, xsend, xrecv):
    me = lax.axis_index("chan")
    inp = lax.axis_index("inp")
    z, y = me // 2, lax.rem(me, 2)
    twin = 2 * z + 1 - y
    mate = inp + 1 - 2 * lax.rem(inp, 2)
    across = lax.rem(inp + 2, 4)

    def far(k):
        return lax.rem(z + k, 4)

    barrier = pltpu.get_barrier_semaphore()
    for other in (twin, 2 * far(1) + y, 2 * far(2) + y, 2 * far(3) + y):
        pl.semaphore_signal(barrier, inc=1, device_id={"chan": other}, device_id_type=MESH)
    for other in (mate, across):
        pl.semaphore_signal(barrier, inc=1, device_id={"inp": other}, device_id_type=MESH)
    pl.semaphore_wait(barrier, 6)

    def first(e):
        return pltpu.make_async_remote_copy(
            src_ref=p_ref.at[1 - y, e, :, pl.ds(0, PART)], dst_ref=near.at[y, e],
            send_sem=ysend.at[e], recv_sem=yrecv.at[e],
            device_id={"chan": twin}, device_id_type=MESH)

    def mine(e):
        return pltpu.make_async_copy(p_ref.at[y, e, :, pl.ds(0, PART)], near.at[y, e], loc_sem.at[e, 0])

    def turn(e, k):
        return pltpu.make_async_remote_copy(
            src_ref=comb.at[e, far(k)], dst_ref=got.at[z, e],
            send_sem=zsend.at[e, k], recv_sem=zrecv.at[e, k],
            device_id={"chan": 2 * far(k) + y}, device_id_type=MESH)

    def stay(e):
        return pltpu.make_async_copy(comb.at[e, z], got.at[z, e], loc_sem.at[e, 1])

    def pair(e, which):
        src = own.at[e] if which < 2 else o_ref.at[across, e]
        dst = o_ref.at[inp, e] if which < 2 else o_ref.at[across, e]
        return pltpu.make_async_remote_copy(
            src_ref=src, dst_ref=dst, send_sem=xsend.at[e, which], recv_sem=xrecv.at[e, which],
            device_id={"inp": across if which == 0 else mate}, device_id_type=MESH)

    def keep(e):
        return pltpu.make_async_copy(own.at[e], o_ref.at[inp, e], loc_sem.at[e, 2])

    def join_twins(e):
        mine(e).wait()
        first(e).wait_recv()

        @pl.loop(0, 4)
        def _(to):
            for j in range(PART + 4):
                total = None
                for src in range(2):
                    if 0 <= j - 4 * src < PART:
                        term = near[src, e, to, j - 4 * src].astype(jnp.float32)
                        total = term if total is None else total + term
                comb[e, to, j] = total.astype(jnp.bfloat16)

        for k in (2, 1, 3):
            turn(e, k).start()
        stay(e).start()

    def join_all(e):
        stay(e).wait()
        for k in range(1, 4):
            turn(e, k).wait_recv()

        @pl.loop(0, 4)
        def _(i):
            r, d0 = i // 2, pl.multiple_of(lax.rem(i, 2) * 16, 16)
            rows = []
            for s in range(32):
                src, j = s // 8, s % 8
                total = got[src, e, j, r, pl.ds(d0, 16), :].astype(jnp.float32)
                if src and j < 7:
                    total = total + got[src - 1, e, j + 8, r, pl.ds(d0, 16), :].astype(jnp.float32)
                rows.append(total)
            lined = jnp.swapaxes(jnp.stack(rows), 0, 1)
            own[e, pl.ds(d0, 16), pl.ds(pl.multiple_of(r * 32, 32), 32), :] = lined.astype(jnp.bfloat16)

        pair(e, 0).start()
        pair(e, 1).start()
        keep(e).start()
        if e:
            pair(e - 1, 0).wait_recv()
            pair(e - 1, 2).start()

    for e in range(SUBS):
        first(e).start()
        mine(e).start()
    join_twins(0)
    join_twins(1)
    join_all(0)
    join_twins(2)
    join_all(1)
    join_twins(3)
    join_all(2)
    join_all(3)
    pair(SUBS - 1, 0).wait_recv()
    pair(SUBS - 1, 2).start()
    for e in range(SUBS):
        first(e).wait_send()
        for k in range(1, 4):
            turn(e, k).wait_send()
        keep(e).wait()
        pair(e, 0).wait_send()
        pair(e, 1).wait()
        pair(e, 2).wait()


def pair_kernel(me_ref, all_ref, own_ref, o_ref):
    del me_ref
    for e in range(4):
        for d in range(2):
            own = own_ref[0, e, d]
            both = jnp.concatenate([jnp.concatenate([own[:32], own[32:]], axis=0),
                                    jnp.concatenate([own[32:], -own[:32]], axis=0)], axis=1)
            every = jnp.concatenate([all_ref[i, e, d] for i in range(4)], axis=1)
            res = lax.dot_general(both, every, (((0,), (0,)), ((), ())), preferred_element_type=jnp.float32)
            res = (res * (1.0 / 32.0)).astype(jnp.bfloat16)
            o_ref[0, 4 * d + e] = res[:128]
            o_ref[1, 4 * d + e] = res[128:]


def fast(voltages, scales):
    wide, even, odd = (jnp.asarray(t) for t in fold_tables())
    gains = (scales.astype(jnp.float32) * (1.0 / 256.0))[:, None]
    whole = lambda *shape: pl.BlockSpec(shape, lambda p: (0,) * len(shape))
    parts = pl.pallas_call(
        front_kernel, grid=(6,),
        out_shape=jax.ShapeDtypeStruct((2, 4, 4, 12, 2, 32, 128), jnp.bfloat16),
        in_specs=[whole(128, 16384), whole(128, 1), whole(16, 1, NFFT), whole(2, 512, 1024), whole(2, 512, 2048)],
        out_specs=pl.BlockSpec((2, 4, 4, 2, 2, 32, 128), lambda p: (0, 0, 0, p, 0, 0, 0)),
        scratch_shapes=[pltpu.VMEM((256, NFFT), jnp.bfloat16)],
        compiler_params=pltpu.CompilerParams(vmem_limit_bytes=56 << 20),
        name="filter_transform",
    )(voltages, gains, wide[:, None], even, odd)
    gathered = pl.pallas_call(
        comm_kernel,
        out_shape=jax.ShapeDtypeStruct((4, SUBS, 32, 64, 128), jnp.bfloat16),
        in_specs=[pl.BlockSpec(memory_space=pl.ANY)],
        out_specs=pl.BlockSpec(memory_space=pl.ANY),
        scratch_shapes=[
            pltpu.VMEM((2, SUBS, 4, PART, 2, 32, 128), jnp.bfloat16),
            pltpu.VMEM((SUBS, 4, PART + 4, 2, 32, 128), jnp.bfloat16),
            pltpu.VMEM((4, SUBS, PART + 4, 2, 32, 128), jnp.bfloat16),
            pltpu.VMEM((SUBS, 32, 64, 128), jnp.bfloat16),
            pltpu.SemaphoreType.DMA((SUBS,)), pltpu.SemaphoreType.DMA((SUBS,)),
            pltpu.SemaphoreType.DMA((SUBS, 4)), pltpu.SemaphoreType.DMA((SUBS, 4)),
            pltpu.SemaphoreType.DMA((SUBS, 3)),
            pltpu.SemaphoreType.DMA((SUBS, 3)), pltpu.SemaphoreType.DMA((SUBS, 3)),
        ],
        compiler_params=pltpu.CompilerParams(
            collective_id=0, has_side_effects=True, vmem_limit_bytes=48 << 20),
        name="turn_and_share",
    )(parts)
    me = lax.axis_index("inp").astype(jnp.int32).reshape(1)
    return pl.pallas_call(
        pair_kernel,
        out_shape=jax.ShapeDtypeStruct((2, 128, 128, 512), jnp.bfloat16),
        grid_spec=pltpu.PrefetchScalarGridSpec(
            num_scalar_prefetch=1, grid=(16,),
            in_specs=[pl.BlockSpec((4, 4, 2, 64, 128), lambda g, m: (0, 0, g, 0, 0)),
                      pl.BlockSpec((1, 4, 2, 64, 128), lambda g, m: (m[0], 0, g, 0, 0))],
            out_specs=pl.BlockSpec((2, 8, 128, 512), lambda g, m: (0, g, 0, 0))),
        compiler_params=pltpu.CompilerParams(vmem_limit_bytes=48 << 20),
        name="correlate",
    )(me, gathered, gathered)


def solution(mesh):
    placed = (P("inp", "chan"), P("inp"))
    sizes = (mesh.shape["chan"], mesh.shape["inp"])
    return jax.shard_map(
        fast if sizes == (8, 4) else shards,
        mesh=mesh, in_specs=placed, out_specs=P(None, "chan", "inp", None), check_vma=False
    )
```

```python
import math

import jax
import jax.numpy as jnp
import ml_dtypes
import numpy as np
from jax import lax
from jax.experimental import pallas as pl
from jax.experimental.pallas import tpu as pltpu
from jax.sharding import PartitionSpec as P

NFFT = 4096
CHANS = 1024
TAPS = 8
MESH = pl.DeviceIdType.MESH


def shifted(block, axis, distance):
    devices = range(lax.axis_size(axis))
    route = [(i - distance, i) for i in devices if i - distance in devices]
    return lax.ppermute(block, axis, route)


def window_table():
    count = TAPS * NFFT
    places = jnp.arange(count).astype(jnp.float32)
    shaping = jnp.sinc((places - count / 2.0) / NFFT)
    taper = 0.5 - 0.5 * jnp.cos(2.0 * math.pi * places / count)
    return (shaping * taper).reshape(TAPS, NFFT)


def dft_table():
    columns = jnp.arange(CHANS, dtype=jnp.int32)
    norm_factor = 1.0 / math.sqrt(NFFT)

    def one_block(start):
        rows_idx = start + jnp.arange(512, dtype=jnp.int32)
        phase = rows_idx[:, None] * columns[None, :] % NFFT
        angle = phase.astype(jnp.float32) * (2.0 * math.pi / NFFT)
        return jnp.stack(
            [jnp.cos(angle) * norm_factor, -jnp.sin(angle) * norm_factor], axis=1
        ).astype(jnp.bfloat16)

    starts = jnp.arange(NFFT // 512, dtype=jnp.int32) * 512
    return lax.map(one_block, starts).reshape(NFFT, 2, CHANS)


def filter_taps(padded, window, spec_count):
    total = jnp.zeros((padded.shape[0], spec_count, NFFT), jnp.float32)
    for tap_index in range(TAPS):
        total = total + window[tap_index] * padded[:, tap_index : tap_index + spec_count]
    return total.astype(jnp.bfloat16)


def shards(voltages, scales):
    inp_count = voltages.shape[0]
    shard_len = voltages.shape[1]
    spec_count = shard_len // NFFT
    history_len = (TAPS - 1) * NFFT
    reach_back = -(-history_len // shard_len)
    samples = voltages.astype(jnp.bfloat16)
    earlier = []
    for distance in range(1, reach_back + 1):
        take_count = min(shard_len, history_len - (distance - 1) * shard_len)
        received = shifted(samples[:, shard_len - take_count :], "chan", distance)
        earlier = [received] + earlier
    joined = jnp.concatenate(earlier + [samples], axis=1).astype(jnp.float32)
    signal = joined * scales.astype(jnp.float32)[:, None] * (1.0 / 256.0)
    padded = signal.reshape(inp_count, TAPS - 1 + spec_count, NFFT)
    filtered = filter_taps(padded, window_table(), spec_count)
    spectra = jnp.einsum(
        "isn,nrc->cirs", filtered, dft_table(), preferred_element_type=jnp.float32
    ).astype(jnp.bfloat16)
    local_block = lax.all_to_all(spectra, "chan", split_axis=0, concat_axis=3, tiled=True)
    chan_count = local_block.shape[0]
    spec_total = local_block.shape[3]
    own_rows = local_block.reshape(chan_count, inp_count, 2 * spec_total)
    swapped = jnp.concatenate([own_rows[..., spec_total:], -own_rows[..., :spec_total]], axis=-1)
    piece = lax.all_gather(own_rows, "inp", axis=1, tiled=True)
    real_part = jnp.einsum("cik,cjk->cij", own_rows, piece, preferred_element_type=jnp.float32)
    imag_part = jnp.einsum("cik,cjk->cij", swapped, piece, preferred_element_type=jnp.float32)
    result = jnp.stack([real_part, imag_part]) * (1.0 / spec_total)
    return result.astype(jnp.bfloat16)


SUBS = 8
PART = 11


def fold_tables():
    places = np.arange(TAPS * NFFT).astype(np.float64)
    window = np.sinc((places - TAPS * NFFT / 2) / NFFT) * (0.5 - 0.5 * np.cos(2 * np.pi * places / (TAPS * NFFT)))
    window = window.reshape(TAPS, NFFT).astype(np.float32)
    wide = np.concatenate([np.zeros((6, NFFT), np.float32), window, np.zeros((4, NFFT), np.float32)], axis=0)
    m = np.arange(NFFT // 4)
    out = []
    for e in range(4):
        c = 4 * np.arange(CHANS // 4) + e
        angle = 2 * np.pi * ((m[None, :] * c[:, None]) % NFFT) / NFFT
        co, si = np.cos(angle) / 64, np.sin(angle) / 64
        if e % 2 == 0:
            re, im = co, -si
        elif e == 1:
            re, im = np.concatenate([co, -si], 1), np.concatenate([-si, -co], 1)
        else:
            re, im = np.concatenate([co, si], 1), np.concatenate([-si, co], 1)
        groups = 8
        both = np.stack([re.reshape(groups, -1, re.shape[1]), im.reshape(groups, -1, re.shape[1])], axis=1)
        out.append(both.reshape(-1, re.shape[1]).astype(ml_dtypes.bfloat16))
    return wide, np.stack([out[0], out[2]]), np.stack([out[1], out[3]])


def front_kernel(x_ref, g_ref, w_ref, even_ref, odd_ref, o_ref, f_ref, new_ref, y_ref):
    p = pl.program_id(0)
    rows, span, quarter = 32, 256, NFFT // 4
    nt = (((1,), (1,)), ((), ()))

    @pl.when(p == 0)
    def _():
        @pl.loop(0, 32)
        def _(i):
            cols = pl.ds(pl.multiple_of(i * 512, 512), 512)
            f_ref[:, cols] = x_ref[:, cols].astype(jnp.float32) * g_ref[...]

    def filter_rows(half, r0):
        s = 2 * p + half
        for l in range(quarter // span):
            f = []
            for q in range(4):
                acc = None
                col = q * quarter + l * span
                for b in range(4):
                    term = f_ref[r0:r0 + rows, b * NFFT + col:b * NFFT + col + span] * w_ref[b + 13 - s, :, col:col + span]
                    acc = term if acc is None else acc + term
                f.append(acc)
            a, b2 = f[0] + f[2], f[1] + f[3]
            at = half * 128 + r0
            for j, v in enumerate((a + b2, a - b2, f[0] - f[2], f[1] - f[3])):
                new_ref[at:at + rows, j * quarter + l * span:j * quarter + (l + 1) * span] = v.astype(jnp.bfloat16)

    for e in range(4):
        filter_rows(0, e * rows)
        filter_rows(1, e * rows)
        for part in range(2):
            sel = pl.ds(part * 256, 256)
            if e % 2 == 0:
                tab, y = even_ref[e // 2, sel, :], y_ref[:, (e // 2) * quarter:(e // 2 + 1) * quarter]
            else:
                tab, y = odd_ref[e // 2, sel, :], y_ref[:, 2 * quarter:]
            res = lax.dot_general(tab, y, nt, preferred_element_type=jnp.float32).astype(jnp.bfloat16)
            for half in range(2):
                blocks = res[:, half * 128:(half + 1) * 128].reshape(2, 2, 2, 2, 16, 128)
                for y_to in range(2):
                    for d in range(2):
                        o_ref[y_to, 2 * e + d, 2 * part:2 * part + 2, half] = blocks[:, y_to, :, d]
    y_ref[...] = new_ref[...]


def comm_kernel(p_ref, o_ref, near, comb, got, own, ysend, yrecv, zsend, zrecv, loc_sem, xsend, xrecv):
    me = lax.axis_index("chan")
    inp = lax.axis_index("inp")
    z, y = me // 2, lax.rem(me, 2)
    twin = 2 * z + 1 - y
    mate = inp + 1 - 2 * lax.rem(inp, 2)
    across = lax.rem(inp + 2, 4)

    def far(k):
        return lax.rem(z + k, 4)

    barrier = pltpu.get_barrier_semaphore()
    for other in (twin, 2 * far(1) + y, 2 * far(2) + y, 2 * far(3) + y):
        pl.semaphore_signal(barrier, inc=1, device_id={"chan": other}, device_id_type=MESH)
    for other in (mate, across):
        pl.semaphore_signal(barrier, inc=1, device_id={"inp": other}, device_id_type=MESH)
    pl.semaphore_wait(barrier, 6)

    def first(e):
        return pltpu.make_async_remote_copy(
            src_ref=p_ref.at[1 - y, e, :, pl.ds(0, PART)], dst_ref=near.at[y, e],
            send_sem=ysend.at[e], recv_sem=yrecv.at[e],
            device_id={"chan": twin}, device_id_type=MESH)

    def mine(e):
        return pltpu.make_async_copy(p_ref.at[y, e, :, pl.ds(0, PART)], near.at[y, e], loc_sem.at[e, 0])

    def turn(e, k):
        return pltpu.make_async_remote_copy(
            src_ref=comb.at[e, far(k)], dst_ref=got.at[z, e],
            send_sem=zsend.at[e, k], recv_sem=zrecv.at[e, k],
            device_id={"chan": 2 * far(k) + y}, device_id_type=MESH)

    def stay(e):
        return pltpu.make_async_copy(comb.at[e, z], got.at[z, e], loc_sem.at[e, 1])

    def pair(e, which):
        src = own.at[e] if which < 2 else o_ref.at[across, e]
        dst = o_ref.at[inp, e] if which < 2 else o_ref.at[across, e]
        return pltpu.make_async_remote_copy(
            src_ref=src, dst_ref=dst, send_sem=xsend.at[e, which], recv_sem=xrecv.at[e, which],
            device_id={"inp": across if which == 0 else mate}, device_id_type=MESH)

    def keep(e):
        return pltpu.make_async_copy(own.at[e], o_ref.at[inp, e], loc_sem.at[e, 2])

    def join_twins(e):
        mine(e).wait()
        first(e).wait_recv()

        @pl.loop(0, 4)
        def _(to):
            for j in range(PART + 4):
                total = None
                for src in range(2):
                    if 0 <= j - 4 * src < PART:
                        term = near[src, e, to, j - 4 * src].astype(jnp.float32)
                        total = term if total is None else total + term
                comb[e, to, j] = total.astype(jnp.bfloat16)

        for k in (2, 1, 3):
            turn(e, k).start()
        stay(e).start()

    def join_all(e):
        stay(e).wait()
        for k in range(1, 4):
            turn(e, k).wait_recv()

        @pl.loop(0, 2)
        def _(r):
            rows = []
            for s in range(32):
                src, j = s // 8, s % 8
                total = got[src, e, j, r].astype(jnp.float32)
                if src and j < 7:
                    total = total + got[src - 1, e, j + 8, r].astype(jnp.float32)
                rows.append(total)
            lined = jnp.swapaxes(jnp.stack(rows), 0, 1)
            own[e, :, pl.ds(pl.multiple_of(r * 32, 32), 32), :] = lined.astype(jnp.bfloat16)

        pair(e, 0).start()
        pair(e, 1).start()
        keep(e).start()
        if e:
            pair(e - 1, 0).wait_recv()
            pair(e - 1, 2).start()

    for e in range(SUBS):
        first(e).start()
        mine(e).start()
    join_twins(0)
    for e in range(1, SUBS):
        join_twins(e)
        join_all(e - 1)
    join_all(SUBS - 1)
    pair(SUBS - 1, 0).wait_recv()
    pair(SUBS - 1, 2).start()
    for e in range(SUBS):
        first(e).wait_send()
        for k in range(1, 4):
            turn(e, k).wait_send()
        keep(e).wait()
        pair(e, 0).wait_send()
        pair(e, 1).wait()
        pair(e, 2).wait()


def pair_kernel(me_ref, all_ref, own_ref, o_ref):
    del me_ref
    for e in range(4):
        for d in range(2):
            own = own_ref[0, e, d] * jnp.bfloat16(1.0 / 32.0)
            turned = jnp.concatenate([own[32:], -own[:32]], axis=0)
            for n in range(2):
                every = jnp.concatenate([all_ref[2 * n, e, d], all_ref[2 * n + 1, e, d]], axis=1)
                for part, left in enumerate((own, turned)):
                    res = lax.dot_general(left, every, (((0,), (0,)), ((), ())), preferred_element_type=jnp.float32)
                    o_ref[part, 4 * d + e, :, n * 256:(n + 1) * 256] = res.astype(jnp.bfloat16)


def fast(voltages, scales):
    wide, even, odd = (jnp.asarray(t) for t in fold_tables())
    gains = (scales.astype(jnp.float32) * (1.0 / 256.0))[:, None]
    whole = lambda *shape: pl.BlockSpec(shape, lambda p: (0,) * len(shape))
    parts = pl.pallas_call(
        front_kernel, grid=(7,),
        out_shape=jax.ShapeDtypeStruct((2, SUBS, 4, 12, 2, 16, 128), jnp.bfloat16),
        in_specs=[whole(128, 16384), whole(128, 1), whole(18, 1, NFFT), whole(2, 512, 1024), whole(2, 512, 2048)],
        out_specs=pl.BlockSpec((2, SUBS, 4, 2, 2, 16, 128), lambda p: (0, 0, 0, jnp.maximum(p - 1, 0), 0, 0, 0)),
        scratch_shapes=[pltpu.VMEM((128, 4 * NFFT), jnp.float32), pltpu.VMEM((256, NFFT), jnp.bfloat16),
                        pltpu.VMEM((256, NFFT), jnp.bfloat16)],
        compiler_params=pltpu.CompilerParams(vmem_limit_bytes=56 << 20),
        name="filter_transform",
    )(voltages, gains, wide[:, None], even, odd)
    gathered = pl.pallas_call(
        comm_kernel,
        out_shape=jax.ShapeDtypeStruct((4, SUBS, 16, 64, 128), jnp.bfloat16),
        in_specs=[pl.BlockSpec(memory_space=pl.ANY)],
        out_specs=pl.BlockSpec(memory_space=pl.ANY),
        scratch_shapes=[
            pltpu.VMEM((2, SUBS, 4, PART, 2, 16, 128), jnp.bfloat16),
            pltpu.VMEM((SUBS, 4, PART + 4, 2, 16, 128), jnp.bfloat16),
            pltpu.VMEM((4, SUBS, PART + 4, 2, 16, 128), jnp.bfloat16),
            pltpu.VMEM((SUBS, 16, 64, 128), jnp.bfloat16),
            pltpu.SemaphoreType.DMA((SUBS,)), pltpu.SemaphoreType.DMA((SUBS,)),
            pltpu.SemaphoreType.DMA((SUBS, 4)), pltpu.SemaphoreType.DMA((SUBS, 4)),
            pltpu.SemaphoreType.DMA((SUBS, 3)),
            pltpu.SemaphoreType.DMA((SUBS, 3)), pltpu.SemaphoreType.DMA((SUBS, 3)),
        ],
        compiler_params=pltpu.CompilerParams(
            collective_id=0, has_side_effects=True, vmem_limit_bytes=48 << 20),
        name="turn_and_share",
    )(parts).reshape(4, 4, 32, 64, 128)
    me = lax.axis_index("inp").astype(jnp.int32).reshape(1)
    return pl.pallas_call(
        pair_kernel,
        out_shape=jax.ShapeDtypeStruct((2, 128, 128, 512), jnp.bfloat16),
        grid_spec=pltpu.PrefetchScalarGridSpec(
            num_scalar_prefetch=1, grid=(16,),
            in_specs=[pl.BlockSpec((4, 4, 2, 64, 128), lambda g, m: (0, 0, g, 0, 0)),
                      pl.BlockSpec((1, 4, 2, 64, 128), lambda g, m: (m[0], 0, g, 0, 0))],
            out_specs=pl.BlockSpec((2, 8, 128, 512), lambda g, m: (0, g, 0, 0))),
        compiler_params=pltpu.CompilerParams(vmem_limit_bytes=48 << 20),
        name="correlate",
    )(me, gathered, gathered)


def solution(mesh):
    placed = (P("inp", "chan"), P("inp"))
    sizes = (mesh.shape["chan"], mesh.shape["inp"])
    return jax.shard_map(
        fast if sizes == (8, 4) else shards,
        mesh=mesh, in_specs=placed, out_specs=P(None, "chan", "inp", None), check_vma=False
    )
```

```python
import math

import jax
import jax.numpy as jnp
import ml_dtypes
import numpy as np
from jax import lax
from jax.experimental import pallas as pl
from jax.experimental.pallas import tpu as pltpu
from jax.sharding import PartitionSpec as P

NFFT = 4096
CHANS = 1024
TAPS = 8
MESH = pl.DeviceIdType.MESH


def shifted(block, axis, distance):
    devices = range(lax.axis_size(axis))
    route = [(i - distance, i) for i in devices if i - distance in devices]
    return lax.ppermute(block, axis, route)


def window_table():
    count = TAPS * NFFT
    places = jnp.arange(count).astype(jnp.float32)
    shaping = jnp.sinc((places - count / 2.0) / NFFT)
    taper = 0.5 - 0.5 * jnp.cos(2.0 * math.pi * places / count)
    return (shaping * taper).reshape(TAPS, NFFT)


def dft_table():
    columns = jnp.arange(CHANS, dtype=jnp.int32)
    norm_factor = 1.0 / math.sqrt(NFFT)

    def one_block(start):
        rows_idx = start + jnp.arange(512, dtype=jnp.int32)
        phase = rows_idx[:, None] * columns[None, :] % NFFT
        angle = phase.astype(jnp.float32) * (2.0 * math.pi / NFFT)
        return jnp.stack(
            [jnp.cos(angle) * norm_factor, -jnp.sin(angle) * norm_factor], axis=1
        ).astype(jnp.bfloat16)

    starts = jnp.arange(NFFT // 512, dtype=jnp.int32) * 512
    return lax.map(one_block, starts).reshape(NFFT, 2, CHANS)


def filter_taps(padded, window, spec_count):
    total = jnp.zeros((padded.shape[0], spec_count, NFFT), jnp.float32)
    for tap_index in range(TAPS):
        total = total + window[tap_index] * padded[:, tap_index : tap_index + spec_count]
    return total.astype(jnp.bfloat16)


def shards(voltages, scales):
    inp_count = voltages.shape[0]
    shard_len = voltages.shape[1]
    spec_count = shard_len // NFFT
    history_len = (TAPS - 1) * NFFT
    reach_back = -(-history_len // shard_len)
    samples = voltages.astype(jnp.bfloat16)
    earlier = []
    for distance in range(1, reach_back + 1):
        take_count = min(shard_len, history_len - (distance - 1) * shard_len)
        received = shifted(samples[:, shard_len - take_count :], "chan", distance)
        earlier = [received] + earlier
    joined = jnp.concatenate(earlier + [samples], axis=1).astype(jnp.float32)
    signal = joined * scales.astype(jnp.float32)[:, None] * (1.0 / 256.0)
    padded = signal.reshape(inp_count, TAPS - 1 + spec_count, NFFT)
    filtered = filter_taps(padded, window_table(), spec_count)
    spectra = jnp.einsum(
        "isn,nrc->cirs", filtered, dft_table(), preferred_element_type=jnp.float32
    ).astype(jnp.bfloat16)
    local_block = lax.all_to_all(spectra, "chan", split_axis=0, concat_axis=3, tiled=True)
    chan_count = local_block.shape[0]
    spec_total = local_block.shape[3]
    own_rows = local_block.reshape(chan_count, inp_count, 2 * spec_total)
    swapped = jnp.concatenate([own_rows[..., spec_total:], -own_rows[..., :spec_total]], axis=-1)
    piece = lax.all_gather(own_rows, "inp", axis=1, tiled=True)
    real_part = jnp.einsum("cik,cjk->cij", own_rows, piece, preferred_element_type=jnp.float32)
    imag_part = jnp.einsum("cik,cjk->cij", swapped, piece, preferred_element_type=jnp.float32)
    result = jnp.stack([real_part, imag_part]) * (1.0 / spec_total)
    return result.astype(jnp.bfloat16)


SUBS = 8
PART = 11


def fold_tables():
    places = np.arange(TAPS * NFFT).astype(np.float64)
    window = np.sinc((places - TAPS * NFFT / 2) / NFFT) * (0.5 - 0.5 * np.cos(2 * np.pi * places / (TAPS * NFFT)))
    window = window.reshape(TAPS, NFFT).astype(np.float32)
    wide = np.concatenate([np.zeros((6, NFFT), np.float32), window, np.zeros((4, NFFT), np.float32)], axis=0)
    m = np.arange(NFFT // 4)
    out = []
    for e in range(4):
        c = 4 * np.arange(CHANS // 4) + e
        angle = 2 * np.pi * ((m[None, :] * c[:, None]) % NFFT) / NFFT
        co, si = np.cos(angle) / 64, np.sin(angle) / 64
        if e % 2 == 0:
            re, im = co, -si
        elif e == 1:
            re, im = np.concatenate([co, -si], 1), np.concatenate([-si, -co], 1)
        else:
            re, im = np.concatenate([co, si], 1), np.concatenate([-si, co], 1)
        groups = 8
        both = np.stack([re.reshape(groups, -1, re.shape[1]), im.reshape(groups, -1, re.shape[1])], axis=1)
        out.append(both.reshape(-1, re.shape[1]).astype(ml_dtypes.bfloat16))
    return wide, np.stack([out[0], out[2]]), np.stack([out[1], out[3]])


def front_kernel(x_ref, g_ref, w_ref, even_ref, odd_ref, o_ref, f_ref, new_ref, y_ref):
    p = pl.program_id(0)
    rows, span, quarter = 32, 256, NFFT // 4
    nt = (((1,), (1,)), ((), ()))

    @pl.when(p == 0)
    def _():
        @pl.loop(0, 32)
        def _(i):
            cols = pl.ds(pl.multiple_of(i * 512, 512), 512)
            f_ref[:, cols] = x_ref[:, cols].astype(jnp.float32) * g_ref[...]

    def filter_rows(half, r0):
        s = 2 * p + half
        for l in range(quarter // span):
            f = []
            for q in range(4):
                acc = None
                col = q * quarter + l * span
                for b in range(4):
                    term = f_ref[r0:r0 + rows, b * NFFT + col:b * NFFT + col + span] * w_ref[b + 13 - s, :, col:col + span]
                    acc = term if acc is None else acc + term
                f.append(acc)
            a, b2 = f[0] + f[2], f[1] + f[3]
            at = half * 128 + r0
            for j, v in enumerate((a + b2, a - b2, f[0] - f[2], f[1] - f[3])):
                new_ref[at:at + rows, j * quarter + l * span:j * quarter + (l + 1) * span] = v.astype(jnp.bfloat16)

    for e in range(4):
        filter_rows(0, e * rows)
        filter_rows(1, e * rows)
        for part in range(2):
            sel = pl.ds(part * 256, 256)
            if e % 2 == 0:
                tab, y = even_ref[e // 2, sel, :], y_ref[:, (e // 2) * quarter:(e // 2 + 1) * quarter]
            else:
                tab, y = odd_ref[e // 2, sel, :], y_ref[:, 2 * quarter:]
            res = lax.dot_general(tab, y, nt, preferred_element_type=jnp.float32).astype(jnp.bfloat16)
            for half in range(2):
                blocks = res[:, half * 128:(half + 1) * 128].reshape(2, 2, 2, 2, 16, 128)
                for y_to in range(2):
                    for d in range(2):
                        o_ref[y_to, 2 * e + d, 2 * part:2 * part + 2, half] = blocks[:, y_to, :, d]
    y_ref[...] = new_ref[...]


def comm_kernel(p_ref, o_ref, near, comb, got, own, passed, ysend, yrecv, zsend, zrecv, loc_sem, xsend, xrecv, rsend, rrecv):
    me = lax.axis_index("chan")
    inp = lax.axis_index("inp")
    z, y = me // 2, lax.rem(me, 2)
    twin = 2 * z + 1 - y
    mate = inp + 1 - 2 * lax.rem(inp, 2)
    across = lax.rem(inp + 2, 4)

    def far(k):
        return lax.rem(z + k, 4)

    barrier = pltpu.get_barrier_semaphore()
    for other in (twin, 2 * far(1) + y, 2 * far(2) + y, 2 * far(3) + y):
        pl.semaphore_signal(barrier, inc=1, device_id={"chan": other}, device_id_type=MESH)
    for other in (mate, across):
        pl.semaphore_signal(barrier, inc=1, device_id={"inp": other}, device_id_type=MESH)
    pl.semaphore_wait(barrier, 6)

    def first(e):
        return pltpu.make_async_remote_copy(
            src_ref=p_ref.at[1 - y, e, :, pl.ds(0, PART)], dst_ref=near.at[y, e],
            send_sem=ysend.at[e], recv_sem=yrecv.at[e],
            device_id={"chan": twin}, device_id_type=MESH)

    def mine(e):
        return pltpu.make_async_copy(p_ref.at[y, e, :, pl.ds(0, PART)], near.at[y, e], loc_sem.at[e, 0])

    def turn(e, k, count):
        return pltpu.make_async_remote_copy(
            src_ref=comb.at[e, far(k), pl.ds(0, count)], dst_ref=got.at[z, e, pl.ds(0, count)],
            send_sem=zsend.at[e, k], recv_sem=zrecv.at[e, k],
            device_id={"chan": 2 * far(k) + y}, device_id_type=MESH)

    def either(source, target, act):
        short = (source == 3) | ((source == 0) & (target >= 2))

        @pl.when(short)
        def _():
            act(8)

        @pl.when(jnp.logical_not(short))
        def _():
            act(PART + 4)

    def relay(e):
        return pltpu.make_async_remote_copy(
            src_ref=comb.at[e, pl.ds(2, 2), pl.ds(8, 7)], dst_ref=passed.at[e],
            send_sem=rsend.at[e], recv_sem=rrecv.at[e],
            device_id={"chan": lax.rem(me + 2, 8)}, device_id_type=MESH)

    def stay(e):
        return pltpu.make_async_copy(comb.at[e, z], got.at[z, e], loc_sem.at[e, 1])

    def pair(e, which):
        src = own.at[e] if which < 2 else o_ref.at[across, e]
        dst = o_ref.at[inp, e] if which < 2 else o_ref.at[across, e]
        return pltpu.make_async_remote_copy(
            src_ref=src, dst_ref=dst, send_sem=xsend.at[e, which], recv_sem=xrecv.at[e, which],
            device_id={"inp": across if which == 0 else mate}, device_id_type=MESH)

    def keep(e):
        return pltpu.make_async_copy(own.at[e], o_ref.at[inp, e], loc_sem.at[e, 2])

    def join_twins(e):
        mine(e).wait()
        first(e).wait_recv()

        @pl.loop(0, 4)
        def _(to):
            for j in range(PART + 4):
                total = None
                for src in range(2):
                    if 0 <= j - 4 * src < PART:
                        term = near[src, e, to, j - 4 * src].astype(jnp.float32)
                        total = term if total is None else total + term
                comb[e, to, j] = total.astype(jnp.bfloat16)

        @pl.when(z == 0)
        def _():
            relay(e).start()

        @pl.when(z == 1)
        def _():
            relay(e).wait_recv()

            @pl.loop(0, 2)
            def _(i):
                for j in range(7):
                    total = comb[e, 2 + i, j].astype(jnp.float32) + passed[e, i, j].astype(jnp.float32)
                    comb[e, 2 + i, j] = total.astype(jnp.bfloat16)

        for k in (2, 1, 3):
            either(z, far(k), lambda count: turn(e, k, count).start())
        stay(e).start()

    def join_all(e):
        stay(e).wait()
        for k in range(1, 4):
            either(far(4 - k), z, lambda count: turn(e, k, count).wait_recv())

        @pl.loop(0, 2)
        def _(r):
            rows = []
            for s in range(32):
                src, j = s // 8, s % 8
                total = got[src, e, j, r].astype(jnp.float32)
                if src and j < 7:
                    total = total + got[src - 1, e, j + 8, r].astype(jnp.float32)
                rows.append(total)
            lined = jnp.swapaxes(jnp.stack(rows), 0, 1)
            own[e, :, pl.ds(pl.multiple_of(r * 32, 32), 32), :] = lined.astype(jnp.bfloat16)

        pair(e, 0).start()
        pair(e, 1).start()
        keep(e).start()
        if e:
            pair(e - 1, 0).wait_recv()
            pair(e - 1, 2).start()

    for e in range(SUBS):
        first(e).start()
        mine(e).start()

    @pl.when(z >= 2)
    def _():
        got[0, :, 8:] = jnp.zeros((SUBS, 7, 2, 16, 128), jnp.bfloat16)

    join_twins(0)
    for e in range(1, SUBS):
        join_twins(e)
        join_all(e - 1)
    join_all(SUBS - 1)
    pair(SUBS - 1, 0).wait_recv()
    pair(SUBS - 1, 2).start()
    @pl.when(z == 0)
    def _():
        for e in range(SUBS):
            relay(e).wait_send()

    for e in range(SUBS):
        first(e).wait_send()
        for k in range(1, 4):
            either(z, far(k), lambda count: turn(e, k, count).wait_send())
        keep(e).wait()
        pair(e, 0).wait_send()
        pair(e, 1).wait()
        pair(e, 2).wait()


def pair_kernel(me_ref, all_ref, own_ref, o_ref):
    del me_ref
    for e in range(4):
        for d in range(2):
            own = own_ref[0, e, d] * jnp.bfloat16(1.0 / 32.0)
            turned = jnp.concatenate([own[32:], -own[:32]], axis=0)
            for n in range(2):
                every = jnp.concatenate([all_ref[2 * n, e, d], all_ref[2 * n + 1, e, d]], axis=1)
                for part, left in enumerate((own, turned)):
                    res = lax.dot_general(left, every, (((0,), (0,)), ((), ())), preferred_element_type=jnp.float32)
                    o_ref[part, 4 * d + e, :, n * 256:(n + 1) * 256] = res.astype(jnp.bfloat16)


def fast(voltages, scales):
    wide, even, odd = (jnp.asarray(t) for t in fold_tables())
    gains = (scales.astype(jnp.float32) * (1.0 / 256.0))[:, None]
    whole = lambda *shape: pl.BlockSpec(shape, lambda p: (0,) * len(shape))
    parts = pl.pallas_call(
        front_kernel, grid=(7,),
        out_shape=jax.ShapeDtypeStruct((2, SUBS, 4, 12, 2, 16, 128), jnp.bfloat16),
        in_specs=[whole(128, 16384), whole(128, 1), whole(18, 1, NFFT), whole(2, 512, 1024), whole(2, 512, 2048)],
        out_specs=pl.BlockSpec((2, SUBS, 4, 2, 2, 16, 128), lambda p: (0, 0, 0, jnp.maximum(p - 1, 0), 0, 0, 0)),
        scratch_shapes=[pltpu.VMEM((128, 4 * NFFT), jnp.float32), pltpu.VMEM((256, NFFT), jnp.bfloat16),
                        pltpu.VMEM((256, NFFT), jnp.bfloat16)],
        compiler_params=pltpu.CompilerParams(vmem_limit_bytes=56 << 20),
        name="filter_transform",
    )(voltages, gains, wide[:, None], even, odd)
    gathered = pl.pallas_call(
        comm_kernel,
        out_shape=jax.ShapeDtypeStruct((4, SUBS, 16, 64, 128), jnp.bfloat16),
        in_specs=[pl.BlockSpec(memory_space=pl.ANY)],
        out_specs=pl.BlockSpec(memory_space=pl.ANY),
        scratch_shapes=[
            pltpu.VMEM((2, SUBS, 4, PART, 2, 16, 128), jnp.bfloat16),
            pltpu.VMEM((SUBS, 4, PART + 4, 2, 16, 128), jnp.bfloat16),
            pltpu.VMEM((4, SUBS, PART + 4, 2, 16, 128), jnp.bfloat16),
            pltpu.VMEM((SUBS, 16, 64, 128), jnp.bfloat16),
            pltpu.VMEM((SUBS, 2, 7, 2, 16, 128), jnp.bfloat16),
            pltpu.SemaphoreType.DMA((SUBS,)), pltpu.SemaphoreType.DMA((SUBS,)),
            pltpu.SemaphoreType.DMA((SUBS, 4)), pltpu.SemaphoreType.DMA((SUBS, 4)),
            pltpu.SemaphoreType.DMA((SUBS, 3)),
            pltpu.SemaphoreType.DMA((SUBS, 3)), pltpu.SemaphoreType.DMA((SUBS, 3)),
            pltpu.SemaphoreType.DMA((SUBS,)), pltpu.SemaphoreType.DMA((SUBS,)),
        ],
        compiler_params=pltpu.CompilerParams(
            collective_id=0, has_side_effects=True, vmem_limit_bytes=48 << 20),
        name="turn_and_share",
    )(parts).reshape(4, 4, 32, 64, 128)
    me = lax.axis_index("inp").astype(jnp.int32).reshape(1)
    return pl.pallas_call(
        pair_kernel,
        out_shape=jax.ShapeDtypeStruct((2, 128, 128, 512), jnp.bfloat16),
        grid_spec=pltpu.PrefetchScalarGridSpec(
            num_scalar_prefetch=1, grid=(16,),
            in_specs=[pl.BlockSpec((4, 4, 2, 64, 128), lambda g, m: (0, 0, g, 0, 0)),
                      pl.BlockSpec((1, 4, 2, 64, 128), lambda g, m: (m[0], 0, g, 0, 0))],
            out_specs=pl.BlockSpec((2, 8, 128, 512), lambda g, m: (0, g, 0, 0))),
        compiler_params=pltpu.CompilerParams(vmem_limit_bytes=48 << 20),
        name="correlate",
    )(me, gathered, gathered)


def solution(mesh):
    placed = (P("inp", "chan"), P("inp"))
    sizes = (mesh.shape["chan"], mesh.shape["inp"])
    return jax.shard_map(
        fast if sizes == (8, 4) else shards,
        mesh=mesh, in_specs=placed, out_specs=P(None, "chan", "inp", None), check_vma=False
    )
```

```python
import math

import jax
import jax.numpy as jnp
import ml_dtypes
import numpy as np
from jax import lax
from jax.experimental import pallas as pl
from jax.experimental.pallas import tpu as pltpu
from jax.sharding import PartitionSpec as P

NFFT = 4096
CHANS = 1024
TAPS = 8
MESH = pl.DeviceIdType.MESH


def shifted(block, axis, distance):
    devices = range(lax.axis_size(axis))
    route = [(i - distance, i) for i in devices if i - distance in devices]
    return lax.ppermute(block, axis, route)


def window_table():
    count = TAPS * NFFT
    places = jnp.arange(count).astype(jnp.float32)
    shaping = jnp.sinc((places - count / 2.0) / NFFT)
    taper = 0.5 - 0.5 * jnp.cos(2.0 * math.pi * places / count)
    return (shaping * taper).reshape(TAPS, NFFT)


def dft_table():
    columns = jnp.arange(CHANS, dtype=jnp.int32)
    norm_factor = 1.0 / math.sqrt(NFFT)

    def one_block(start):
        rows_idx = start + jnp.arange(512, dtype=jnp.int32)
        phase = rows_idx[:, None] * columns[None, :] % NFFT
        angle = phase.astype(jnp.float32) * (2.0 * math.pi / NFFT)
        return jnp.stack(
            [jnp.cos(angle) * norm_factor, -jnp.sin(angle) * norm_factor], axis=1
        ).astype(jnp.bfloat16)

    starts = jnp.arange(NFFT // 512, dtype=jnp.int32) * 512
    return lax.map(one_block, starts).reshape(NFFT, 2, CHANS)


def filter_taps(padded, window, spec_count):
    total = jnp.zeros((padded.shape[0], spec_count, NFFT), jnp.float32)
    for tap_index in range(TAPS):
        total = total + window[tap_index] * padded[:, tap_index : tap_index + spec_count]
    return total.astype(jnp.bfloat16)


def shards(voltages, scales):
    inp_count = voltages.shape[0]
    shard_len = voltages.shape[1]
    spec_count = shard_len // NFFT
    history_len = (TAPS - 1) * NFFT
    reach_back = -(-history_len // shard_len)
    samples = voltages.astype(jnp.bfloat16)
    earlier = []
    for distance in range(1, reach_back + 1):
        take_count = min(shard_len, history_len - (distance - 1) * shard_len)
        received = shifted(samples[:, shard_len - take_count :], "chan", distance)
        earlier = [received] + earlier
    joined = jnp.concatenate(earlier + [samples], axis=1).astype(jnp.float32)
    signal = joined * scales.astype(jnp.float32)[:, None] * (1.0 / 256.0)
    padded = signal.reshape(inp_count, TAPS - 1 + spec_count, NFFT)
    filtered = filter_taps(padded, window_table(), spec_count)
    spectra = jnp.einsum(
        "isn,nrc->cirs", filtered, dft_table(), preferred_element_type=jnp.float32
    ).astype(jnp.bfloat16)
    local_block = lax.all_to_all(spectra, "chan", split_axis=0, concat_axis=3, tiled=True)
    chan_count = local_block.shape[0]
    spec_total = local_block.shape[3]
    own_rows = local_block.reshape(chan_count, inp_count, 2 * spec_total)
    swapped = jnp.concatenate([own_rows[..., spec_total:], -own_rows[..., :spec_total]], axis=-1)
    piece = lax.all_gather(own_rows, "inp", axis=1, tiled=True)
    real_part = jnp.einsum("cik,cjk->cij", own_rows, piece, preferred_element_type=jnp.float32)
    imag_part = jnp.einsum("cik,cjk->cij", swapped, piece, preferred_element_type=jnp.float32)
    result = jnp.stack([real_part, imag_part]) * (1.0 / spec_total)
    return result.astype(jnp.bfloat16)


SUBS = 8
PART = 11


def fold_tables():
    places = np.arange(TAPS * NFFT).astype(np.float64)
    window = np.sinc((places - TAPS * NFFT / 2) / NFFT) * (0.5 - 0.5 * np.cos(2 * np.pi * places / (TAPS * NFFT)))
    window = window.reshape(TAPS, NFFT).astype(np.float32)
    wide = np.concatenate([np.zeros((6, NFFT), np.float32), window, np.zeros((4, NFFT), np.float32)], axis=0)
    m = np.arange(NFFT // 4)
    out = []
    for e in range(4):
        c = 4 * np.arange(CHANS // 4) + e
        angle = 2 * np.pi * ((m[None, :] * c[:, None]) % NFFT) / NFFT
        co, si = np.cos(angle) / 64, np.sin(angle) / 64
        if e % 2 == 0:
            re, im = co, -si
        elif e == 1:
            re, im = np.concatenate([co, -si], 1), np.concatenate([-si, -co], 1)
        else:
            re, im = np.concatenate([co, si], 1), np.concatenate([-si, co], 1)
        groups = 8
        both = np.stack([re.reshape(groups, -1, re.shape[1]), im.reshape(groups, -1, re.shape[1])], axis=1)
        out.append(both.reshape(-1, re.shape[1]).astype(ml_dtypes.bfloat16))
    return wide, np.stack([out[0], out[2]]), np.stack([out[1], out[3]])


def front_kernel(x_ref, g_ref, w_ref, even_ref, odd_ref, o_ref, f_ref, y_ref):
    p = pl.program_id(0)
    rows, span, quarter = 32, 256, NFFT // 4
    nt = (((1,), (1,)), ((), ()))

    @pl.when(p == 0)
    def _():
        @pl.loop(0, 32)
        def _(i):
            cols = pl.ds(pl.multiple_of(i * 512, 512), 512)
            f_ref[:, cols] = x_ref[:, cols].astype(jnp.float32) * g_ref[...]

    def filter_rows(half, r0):
        s = 2 * p + half
        for l in range(quarter // span):
            f = []
            for q in range(4):
                acc = None
                col = q * quarter + l * span
                for b in range(4):
                    term = f_ref[r0:r0 + rows, b * NFFT + col:b * NFFT + col + span] * w_ref[b + 13 - s, :, col:col + span]
                    acc = term if acc is None else acc + term
                f.append(acc)
            a, b2 = f[0] + f[2], f[1] + f[3]
            at = half * 128 + r0
            for j, v in enumerate((a + b2, a - b2, f[0] - f[2], f[1] - f[3])):
                y_ref[at:at + rows, j * quarter + l * span:j * quarter + (l + 1) * span] = v.astype(jnp.bfloat16)

    for chunk in range(4):
        filter_rows(0, chunk * rows)
        filter_rows(1, chunk * rows)
    for e in range(4):
        for part in range(2):
            sel = pl.ds(part * 256, 256)
            if e % 2 == 0:
                tab, y = even_ref[e // 2, sel, :], y_ref[:, (e // 2) * quarter:(e // 2 + 1) * quarter]
            else:
                tab, y = odd_ref[e // 2, sel, :], y_ref[:, 2 * quarter:]
            res = lax.dot_general(tab, y, nt, preferred_element_type=jnp.float32).astype(jnp.bfloat16)
            for half in range(2):
                blocks = res[:, half * 128:(half + 1) * 128].reshape(2, 2, 2, 2, 16, 128)
                for y_to in range(2):
                    for d in range(2):
                        o_ref[y_to, 2 * e + d, 2 * part:2 * part + 2, half] = blocks[:, y_to, :, d]


def comm_kernel(p_ref, o_ref, near, comb, got, own, passed, ysend, yrecv, zsend, zrecv, loc_sem, xsend, xrecv, rsend, rrecv):
    me = lax.axis_index("chan")
    inp = lax.axis_index("inp")
    z, y = me // 2, lax.rem(me, 2)
    twin = 2 * z + 1 - y
    mate = inp + 1 - 2 * lax.rem(inp, 2)
    across = lax.rem(inp + 2, 4)

    def far(k):
        return lax.rem(z + k, 4)

    barrier = pltpu.get_barrier_semaphore()
    for other in (twin, 2 * far(1) + y, 2 * far(2) + y, 2 * far(3) + y):
        pl.semaphore_signal(barrier, inc=1, device_id={"chan": other}, device_id_type=MESH)
    for other in (mate, across):
        pl.semaphore_signal(barrier, inc=1, device_id={"inp": other}, device_id_type=MESH)
    pl.semaphore_wait(barrier, 6)

    def first(e):
        return pltpu.make_async_remote_copy(
            src_ref=p_ref.at[1 - y, e, :, pl.ds(0, PART)], dst_ref=near.at[y, e],
            send_sem=ysend.at[e], recv_sem=yrecv.at[e],
            device_id={"chan": twin}, device_id_type=MESH)

    def mine(e):
        return pltpu.make_async_copy(p_ref.at[y, e, :, pl.ds(0, PART)], near.at[y, e], loc_sem.at[e, 0])

    def turn(e, k, count):
        return pltpu.make_async_remote_copy(
            src_ref=comb.at[e, far(k), pl.ds(0, count)], dst_ref=got.at[z, e, pl.ds(0, count)],
            send_sem=zsend.at[e, k], recv_sem=zrecv.at[e, k],
            device_id={"chan": 2 * far(k) + y}, device_id_type=MESH)

    def either(source, target, act):
        short = (source == 3) | ((source == 0) & (target >= 2))

        @pl.when(short)
        def _():
            act(8)

        @pl.when(jnp.logical_not(short))
        def _():
            act(PART + 4)

    def relay(e):
        return pltpu.make_async_remote_copy(
            src_ref=comb.at[e, pl.ds(2, 2), pl.ds(8, 7)], dst_ref=passed.at[e],
            send_sem=rsend.at[e], recv_sem=rrecv.at[e],
            device_id={"chan": lax.rem(me + 2, 8)}, device_id_type=MESH)

    def stay(e):
        return pltpu.make_async_copy(comb.at[e, z], got.at[z, e], loc_sem.at[e, 1])

    def pair(e, which):
        src = own.at[e] if which < 2 else o_ref.at[across, e]
        dst = o_ref.at[inp, e] if which < 2 else o_ref.at[across, e]
        return pltpu.make_async_remote_copy(
            src_ref=src, dst_ref=dst, send_sem=xsend.at[e, which], recv_sem=xrecv.at[e, which],
            device_id={"inp": across if which == 0 else mate}, device_id_type=MESH)

    def keep(e):
        return pltpu.make_async_copy(own.at[e], o_ref.at[inp, e], loc_sem.at[e, 2])

    def join_twins(e):
        mine(e).wait()
        first(e).wait_recv()

        @pl.loop(0, 4)
        def _(to):
            for j in range(PART + 4):
                total = None
                for src in range(2):
                    if 0 <= j - 4 * src < PART:
                        term = near[src, e, to, j - 4 * src].astype(jnp.float32)
                        total = term if total is None else total + term
                comb[e, to, j] = total.astype(jnp.bfloat16)

        @pl.when(z == 0)
        def _():
            relay(e).start()

        @pl.when(z == 1)
        def _():
            relay(e).wait_recv()

            @pl.loop(0, 2)
            def _(i):
                for j in range(7):
                    total = comb[e, 2 + i, j].astype(jnp.float32) + passed[e, i, j].astype(jnp.float32)
                    comb[e, 2 + i, j] = total.astype(jnp.bfloat16)

        for k in (2, 1, 3):
            either(z, far(k), lambda count: turn(e, k, count).start())
        stay(e).start()

    def join_all(e):
        stay(e).wait()
        for k in range(1, 4):
            either(far(4 - k), z, lambda count: turn(e, k, count).wait_recv())

        @pl.loop(0, 2)
        def _(r):
            rows = []
            for s in range(32):
                src, j = s // 8, s % 8
                total = got[src, e, j, r].astype(jnp.float32)
                if src and j < 7:
                    total = total + got[src - 1, e, j + 8, r].astype(jnp.float32)
                rows.append(total)
            lined = jnp.swapaxes(jnp.stack(rows), 0, 1)
            own[e, :, pl.ds(pl.multiple_of(r * 32, 32), 32), :] = lined.astype(jnp.bfloat16)

        pair(e, 0).start()
        pair(e, 1).start()
        keep(e).start()
        if e:
            pair(e - 1, 0).wait_recv()
            pair(e - 1, 2).start()

    for e in range(SUBS):
        first(e).start()
        mine(e).start()

    @pl.when(z >= 2)
    def _():
        got[0, :, 8:] = jnp.zeros((SUBS, 7, 2, 16, 128), jnp.bfloat16)

    join_twins(0)
    for e in range(1, SUBS):
        join_twins(e)
        join_all(e - 1)
    join_all(SUBS - 1)
    pair(SUBS - 1, 0).wait_recv()
    pair(SUBS - 1, 2).start()
    @pl.when(z == 0)
    def _():
        for e in range(SUBS):
            relay(e).wait_send()

    for e in range(SUBS):
        first(e).wait_send()
        for k in range(1, 4):
            either(z, far(k), lambda count: turn(e, k, count).wait_send())
        keep(e).wait()
        pair(e, 0).wait_send()
        pair(e, 1).wait()
        pair(e, 2).wait()


def pair_kernel(me_ref, all_ref, o_ref):
    me = me_ref[0]
    for e in range(4):
        for d in range(4):
            own = all_ref[me, e, d] * jnp.bfloat16(1.0 / 32.0)
            turned = jnp.concatenate([own[32:], -own[:32]], axis=0)
            for n in range(2):
                every = jnp.concatenate([all_ref[2 * n, e, d], all_ref[2 * n + 1, e, d]], axis=1)
                for part, left in enumerate((own, turned)):
                    res = lax.dot_general(left, every, (((0,), (0,)), ((), ())), preferred_element_type=jnp.float32)
                    o_ref[part, 4 * d + e, :, n * 256:(n + 1) * 256] = res.astype(jnp.bfloat16)


def fast(voltages, scales):
    wide, even, odd = (jnp.asarray(t) for t in fold_tables())
    gains = (scales.astype(jnp.float32) * (1.0 / 256.0))[:, None]
    whole = lambda *shape: pl.BlockSpec(shape, lambda p: (0,) * len(shape))
    parts = pl.pallas_call(
        front_kernel, grid=(6,),
        out_shape=jax.ShapeDtypeStruct((2, SUBS, 4, 12, 2, 16, 128), jnp.bfloat16),
        in_specs=[whole(128, 16384), whole(128, 1), whole(18, 1, NFFT), whole(2, 512, 1024), whole(2, 512, 2048)],
        out_specs=pl.BlockSpec((2, SUBS, 4, 2, 2, 16, 128), lambda p: (0, 0, 0, p, 0, 0, 0)),
        scratch_shapes=[pltpu.VMEM((128, 4 * NFFT), jnp.float32), pltpu.VMEM((256, NFFT), jnp.bfloat16)],
        compiler_params=pltpu.CompilerParams(vmem_limit_bytes=56 << 20),
        name="filter_transform",
    )(voltages, gains, wide[:, None], even, odd)
    gathered = pl.pallas_call(
        comm_kernel,
        out_shape=jax.ShapeDtypeStruct((4, SUBS, 16, 64, 128), jnp.bfloat16),
        in_specs=[pl.BlockSpec(memory_space=pl.ANY)],
        out_specs=pl.BlockSpec(memory_space=pl.ANY),
        scratch_shapes=[
            pltpu.VMEM((2, SUBS, 4, PART, 2, 16, 128), jnp.bfloat16),
            pltpu.VMEM((SUBS, 4, PART + 4, 2, 16, 128), jnp.bfloat16),
            pltpu.VMEM((4, SUBS, PART + 4, 2, 16, 128), jnp.bfloat16),
            pltpu.VMEM((SUBS, 16, 64, 128), jnp.bfloat16),
            pltpu.VMEM((SUBS, 2, 7, 2, 16, 128), jnp.bfloat16),
            pltpu.SemaphoreType.DMA((SUBS,)), pltpu.SemaphoreType.DMA((SUBS,)),
            pltpu.SemaphoreType.DMA((SUBS, 4)), pltpu.SemaphoreType.DMA((SUBS, 4)),
            pltpu.SemaphoreType.DMA((SUBS, 3)),
            pltpu.SemaphoreType.DMA((SUBS, 3)), pltpu.SemaphoreType.DMA((SUBS, 3)),
            pltpu.SemaphoreType.DMA((SUBS,)), pltpu.SemaphoreType.DMA((SUBS,)),
        ],
        compiler_params=pltpu.CompilerParams(
            collective_id=0, has_side_effects=True, vmem_limit_bytes=48 << 20),
        name="turn_and_share",
    )(parts).reshape(4, 4, 32, 64, 128)
    me = lax.axis_index("inp").astype(jnp.int32).reshape(1)
    return pl.pallas_call(
        pair_kernel,
        out_shape=jax.ShapeDtypeStruct((2, 128, 128, 512), jnp.bfloat16),
        grid_spec=pltpu.PrefetchScalarGridSpec(
            num_scalar_prefetch=1, grid=(8,),
            in_specs=[pl.BlockSpec((4, 4, 4, 64, 128), lambda g, m: (0, 0, g, 0, 0))],
            out_specs=pl.BlockSpec((2, 16, 128, 512), lambda g, m: (0, g, 0, 0))),
        compiler_params=pltpu.CompilerParams(vmem_limit_bytes=48 << 20),
        name="correlate",
    )(me, gathered)


def solution(mesh):
    placed = (P("inp", "chan"), P("inp"))
    sizes = (mesh.shape["chan"], mesh.shape["inp"])
    return jax.shard_map(
        fast if sizes == (8, 4) else shards,
        mesh=mesh, in_specs=placed, out_specs=P(None, "chan", "inp", None), check_vma=False
    )
```
